32 devices in a mesh: seq: 8 (over y, x, core), fsdp: 4 (over z).
Axes of the slice: x: 2, y: 2, z: 4, core: 2. Of those that a mesh axis runs over, the one named last changes fastest.
Arguments:
- queries: bfloat16 [2048, 3072], P('seq', 'fsdp'), may hold values from -64 to 64
- key_rows: bfloat16 [2048, 3072], P('seq', 'fsdp'), may hold values from -4 to 4
- value_rows: bfloat16 [2048, 3072], P('seq', 'fsdp'), may hold values from -6 to 6
- pattern: int32 [16, 8], P('seq'), may hold values from 0 to 15, as said below
- out_weight: bfloat16 [128, 24, 6144], P('seq', None, 'fsdp'), may hold values from -0.109375 to 0.109375
- out_grad: bfloat16 [2048, 6144], P('seq', 'fsdp'), may hold values from -6 to 6
Outputs:
- projected: bfloat16 [2048, 6144], P('seq', 'fsdp')
- query_grad: bfloat16 [2048, 3072], P('seq', 'fsdp')
- key_grad: bfloat16 [2048, 3072], P('seq', 'fsdp')
- value_grad: bfloat16 [2048, 3072], P('seq', 'fsdp')
- weight_grad: float32 [128, 24, 6144], P('seq', None, 'fsdp')
The draws below stay inside these ranges and needn't reach their ends.
Inputs may be any that keep to these rules, and one draw needn't show every extreme that they name: `pattern`: row i holds (i - 1) mod 16, i and (i + 1) mod 16 in columns 0 to 2; columns 3 and 4 hold the same two different blocks in every row; in columns 5 to 7, the 2 rows from any multiple of 2 name blocks of any one range o * 2 to (o + 1) * 2 - 1 at most 1 times together, and some range exactly 1 times.
All inputs are finite; a program needn't handle non-finite values.
Results may differ from the reference program's by a relative error of at most 0.035.
Values may be sent and summed in bfloat16 or wider, within the bound.
A program may use at most 128 MiB of HBM per device.

```python
import math
import jax
import jax.numpy as jnp
from jax import lax

D = 6144
HEADS = 24
HD = 128
BLK = 128
NRAND = 3
QB_DEV = 2
NSEL = 8
NBLK = 16
TOKENS = 2048
N_SEQ = 8
N_FSDP = 4


def paired_draw(key):
    base_key = jax.random.fold_in(key, 71)
    first_key, second_key = jax.random.split(base_key)
    full_shape = (TOKENS, HEADS * HD)
    keys_out = jnp.clip(jax.random.normal(first_key, full_shape, jnp.float32), -4.0, 4.0)
    queries_out = jnp.clip(jax.random.normal(second_key, full_shape, jnp.float32), -4.0, 4.0)
    return (queries_out, keys_out)


def draw_queries(key, part):
    queries_out, keys_out = paired_draw(key)
    return queries_out.astype(jnp.bfloat16)


def draw_key_rows(key, part):
    queries_out, keys_out = paired_draw(key)
    return keys_out.astype(jnp.bfloat16)


def draw_pattern(key, part):
    owner_total = NBLK // QB_DEV
    block_ids = jnp.arange(NBLK, dtype=jnp.int32)
    before = (block_ids - 1 + NBLK) % NBLK
    after = (block_ids + 1) % NBLK
    key_first, key_second, key_perm, key_within = jax.random.split(jax.random.fold_in(key, 5), 4)
    first_global = jax.random.randint(key_first, (), 0, NBLK, dtype=jnp.int32)
    second_global = (first_global + jax.random.randint(key_second, (), 1, NBLK, dtype=jnp.int32)) % NBLK
    owner_keys = jax.random.split(key_perm, owner_total)
    orders = jax.vmap(lambda one_key: jax.random.permutation(one_key, owner_total))(owner_keys).astype(jnp.int32)
    request_pos = jnp.arange(QB_DEV * NRAND, dtype=jnp.int32) % owner_total
    owners = orders[:, request_pos]
    within = jax.random.randint(key_within, (owner_total, QB_DEV * NRAND), 0, QB_DEV, dtype=jnp.int32)
    picks = (owners * QB_DEV + within).reshape(NBLK, NRAND)
    globals_col = jnp.stack([jnp.full((NBLK,), first_global, jnp.int32), jnp.full((NBLK,), second_global, jnp.int32)], axis=1)
    return jnp.concatenate([jnp.stack([before, block_ids, after], axis=1), globals_col, picks], axis=1).astype(jnp.int32)


def levels(stream_key, shape, cuts, least, top_value):
    factor_of, own = 1.0, jax.random.fold_in(stream_key, 6)
    for dim, parts in cuts:
        steps = jnp.exp(jax.random.uniform(jax.random.fold_in(own, dim), (parts,), jnp.float32, least / len(cuts), top_value / len(cuts)))
        factor_of = factor_of * jnp.repeat(steps, shape[dim] // parts).reshape([-1 if axis == dim else 1 for axis in range(len(shape))])
    return factor_of


def centred(key, extent, deviation, limit, pieces=(), kind=jnp.bfloat16):
    factor_of = levels(key, extent, pieces, -0.22, 0.18) if pieces else 1.0
    values = jax.random.normal(key, extent, jnp.float32) * deviation * factor_of
    return jnp.minimum(jnp.maximum(values, -limit), limit).astype(kind)


def setup_inputs(seed: int = 0) -> dict:
    keys = jax.random.split(jax.random.key(seed), 7)
    return {
        "queries": draw_queries(jax.random.fold_in(keys[6], 71), 0),
        "key_rows": draw_key_rows(jax.random.fold_in(keys[6], 71), 0),
        "value_rows": centred(keys[2], (TOKENS, HEADS * HD), 1.0, 6.0, ((0, 8), (1, 4))),
        "pattern": draw_pattern(jax.random.fold_in(keys[6], 71), 0),
        "out_weight": centred(keys[4], (HD, HEADS, D), (HEADS * HD) ** -0.5, 0.109375, ((0, 8), (2, 4))),
        "out_grad": centred(keys[5], (TOKENS, D), 1.0, 6.0, ((0, 8), (1, 4))),
    }


HIGH = lax.Precision.HIGHEST

def as_float(array):
    return array.astype(jnp.float32)

def block_probs(query_block, key_set, score_scale):
    scores = jnp.einsum('qhd,khd->hqk', as_float(query_block), as_float(key_set), precision=HIGH) * score_scale
    probs = jax.nn.softmax(scores, axis=-1)
    return (probs, probs.astype(jnp.bfloat16))

def reference(queries, key_rows, value_rows, pattern, out_weight, out_grad):
    tok_total, width_all = queries.shape
    heads_all = width_all // HD
    block_total = tok_total // BLK
    score_scale = 1.0 / math.sqrt(HD)
    query_blocks = queries.reshape(block_total, BLK, heads_all, HD)
    key_blocks = key_rows.reshape(block_total, BLK, heads_all, HD)
    value_blocks = value_rows.reshape(block_total, BLK, heads_all, HD)

    def gather_set(blocks_in, picks):
        return jnp.take(blocks_in, picks, axis=0).reshape(NSEL * BLK, heads_all, HD)

    def attend(inputs):
        query_block, picks = inputs
        key_set = gather_set(key_blocks, picks)
        value_set = gather_set(value_blocks, picks)
        probs, probs_low = block_probs(query_block, key_set, score_scale)
        output = jnp.einsum('hqk,khd->qhd', as_float(probs_low), as_float(value_set), precision=HIGH)
        return output.astype(jnp.bfloat16)
    attended = lax.map(attend, (query_blocks, pattern)).reshape(tok_total, heads_all, HD)
    projected = jnp.einsum('the,ehc->tc', as_float(attended), as_float(out_weight), precision=HIGH).astype(jnp.bfloat16)
    group_cols = out_weight.shape[2] // N_FSDP
    head_grad = jnp.zeros((tok_total, heads_all, HD), jnp.float32)
    for group_index in range(N_FSDP):
        col_start = group_index * group_cols
        grad_cols = out_grad[:, col_start:col_start + group_cols]
        weight_cols = out_weight[:, :, col_start:col_start + group_cols]
        part_sum = jnp.einsum('tc,ehc->the', as_float(grad_cols), as_float(weight_cols), precision=HIGH)
        head_grad = head_grad + lax.optimization_barrier(part_sum.astype(jnp.bfloat16)).astype(jnp.float32)
    head_grad = head_grad.astype(jnp.bfloat16)
    owner_rows = tok_total // N_SEQ
    attended_owner = attended.reshape(N_SEQ, owner_rows, heads_all, HD)
    grad_owner = out_grad.reshape(N_SEQ, owner_rows, out_grad.shape[1])

    def add_owner(total, inputs):
        attn_part, grad_part = inputs
        term = jnp.einsum('the,tc->ehc', as_float(attn_part), as_float(grad_part), precision=HIGH)
        return (total + lax.optimization_barrier(term.astype(jnp.bfloat16)).astype(jnp.float32), None)
    weight_grad, unused = lax.scan(add_owner, jnp.zeros(out_weight.shape, jnp.float32), (attended_owner, grad_owner))
    grad_blocks = head_grad.reshape(block_total, BLK, heads_all, HD)

    def backward_block(carry, inputs):
        key_acc, value_acc = carry
        query_block, grad_block, picks = inputs
        key_set = gather_set(key_blocks, picks)
        value_set = gather_set(value_blocks, picks)
        probs, probs_low = block_probs(query_block, key_set, score_scale)
        prob_grad = jnp.einsum('qhd,khd->hqk', as_float(grad_block), as_float(value_set), precision=HIGH)
        center = lax.optimization_barrier(jnp.sum(probs * prob_grad, axis=-1, keepdims=True))
        score_grad = (probs * (prob_grad - center)).astype(jnp.bfloat16)
        query_out = (jnp.einsum('hqk,khd->qhd', as_float(score_grad), as_float(key_set), precision=HIGH) * score_scale).astype(jnp.bfloat16)
        key_terms = (jnp.einsum('hqk,qhd->khd', as_float(score_grad), as_float(query_block), precision=HIGH) * score_scale).astype(jnp.bfloat16)
        value_terms = jnp.einsum('hqk,qhd->khd', as_float(probs_low), as_float(grad_block), precision=HIGH).astype(jnp.bfloat16)
        key_acc = key_acc.at[picks].add(as_float(key_terms).reshape(NSEL, BLK, heads_all * HD))
        value_acc = value_acc.at[picks].add(as_float(value_terms).reshape(NSEL, BLK, heads_all * HD))
        return ((key_acc, value_acc), query_out)
    zero_acc = jnp.zeros((block_total, BLK, heads_all * HD), jnp.float32)
    (key_acc, value_acc), query_grad = lax.scan(backward_block, (zero_acc, zero_acc), (query_blocks, grad_blocks, pattern))
    query_grad = query_grad.reshape(tok_total, width_all)
    key_grad = key_acc.astype(jnp.bfloat16).reshape(tok_total, width_all)
    value_grad = value_acc.astype(jnp.bfloat16).reshape(tok_total, width_all)
    return (projected, query_grad, key_grad, value_grad, weight_grad)
```

```python
import functools
import math

import jax
import jax.numpy as jnp
from jax import lax
from jax.experimental import pallas as pl
from jax.experimental.pallas import tpu as pltpu
from jax.sharding import PartitionSpec as P

HD = 128
BLK = 128
NSEL = 8
MESH = pl.DeviceIdType.MESH
ANY = pl.BlockSpec(memory_space=pl.ANY)
VMEM = pl.BlockSpec(memory_space=pltpu.VMEM)
DMA = pltpu.SemaphoreType.DMA
CHUNK = 32


def remote(src, dst, send_sem, recv_sem, **where):
    return pltpu.make_async_remote_copy(
        src_ref=src,
        dst_ref=dst,
        send_sem=send_sem,
        recv_sem=recv_sem,
        device_id=where,
        device_id_type=MESH,
    )


def chip_place():
    me = lax.axis_index("seq")
    core = lax.rem(me, 2)
    chip = me // 2
    return me, chip, core, chip * 2 + 1 - core


def greet(seq_all, count, fsdp_count):
    me, chip, core, partner = chip_place()
    barrier = pltpu.get_barrier_semaphore()
    total = 0
    if seq_all:
        for k in range(1, count):
            pl.semaphore_signal(
                barrier, inc=1, device_id={"seq": lax.rem(me + k, count)}, device_id_type=MESH
            )
            total += 1
    else:
        pl.semaphore_signal(barrier, inc=1, device_id={"seq": partner}, device_id_type=MESH)
        total += 1
        for k in range(1, count // 2):
            other = lax.rem(chip + k, count // 2) * 2 + core
            pl.semaphore_signal(barrier, inc=1, device_id={"seq": other}, device_id_type=MESH)
            total += 1
    if fsdp_count:
        mine = lax.axis_index("fsdp")
        for k in range(1, fsdp_count):
            other = lax.rem(mine + k, fsdp_count)
            pl.semaphore_signal(barrier, inc=1, device_id={"fsdp": other}, device_id_type=MESH)
            total += 1
    pl.semaphore_wait(barrier, total)


class Gather:
    def __init__(self, count, x, out, send, recv, near_send, near_recv, local):
        self.n = count // 2
        self.x, self.out = x, out
        self.send, self.recv = send, recv
        self.near_send, self.near_recv, self.local = near_send, near_recv, local

    def far(self, k):
        me, chip, core, partner = chip_place()
        other = lax.rem(chip + k, self.n) * 2 + core
        return remote(self.x, self.out.at[me], self.send.at[k], self.recv.at[k], seq=other)

    def near(self, k):
        me, chip, core, partner = chip_place()
        slot = lax.rem(chip + self.n - k, self.n) * 2 + core
        src = self.x if k == 0 else self.out.at[slot]
        return remote(src, self.out.at[slot], self.near_send.at[k], self.near_recv.at[k], seq=partner)

    def start(self):
        me = lax.axis_index("seq")
        for k in range(1, self.n):
            self.far(k).start()
        self.near(0).start()
        self.own = pltpu.make_async_copy(self.x, self.out.at[me], self.local)
        self.own.start()

    def forward(self):
        for k in range(1, self.n):
            self.far(k).wait_recv()
            self.near(k).start()

    def finish(self):
        self.own.wait()
        for k in range(1, self.n):
            self.far(k).wait_send()
        for k in range(self.n):
            self.near(k).wait_send()
            self.near(k).wait_recv()


class Scatter:
    def __init__(self, count, x, out, got, staged, arrived, send, recv, near_send, near_recv):
        self.n = count // 2
        self.x, self.out, self.got, self.staged, self.arrived = x, out, got, staged, arrived
        self.send, self.recv, self.near_send, self.near_recv = send, recv, near_send, near_recv

    def near(self, k):
        me, chip, core, partner = chip_place()
        slot = lax.rem(chip + k, self.n) * 2 + 1 - core
        return remote(
            self.x.at[slot], self.got.at[k], self.near_send.at[k], self.near_recv.at[k], seq=partner
        )

    def far(self, k):
        me, chip, core, partner = chip_place()
        other = lax.rem(chip + k, self.n) * 2 + core
        return remote(
            self.staged.at[k], self.arrived.at[k], self.send.at[k], self.recv.at[k], seq=other
        )

    def start(self):
        for k in list(range(1, self.n)) + [0]:
            self.near(k).start()

    def exchange(self, k):
        me, chip, core, partner = chip_place()
        slot = lax.rem(chip + k, self.n) * 2 + core
        self.near(k).wait_recv()

        def body(i, carry):
            rows = pl.ds(pl.multiple_of(i * CHUNK, CHUNK), CHUNK)
            total = self.x[slot, rows, :].astype(jnp.float32) + self.got[k, rows, :].astype(
                jnp.float32
            )
            self.staged[k, rows, :] = total.astype(jnp.bfloat16)
            return carry

        lax.fori_loop(0, self.x.shape[1] // CHUNK, body, 0)
        if k:
            self.far(k).start()

    def finish(self):
        for k in range(1, self.n):
            self.far(k).wait_recv()

        def body(i, carry):
            rows = pl.ds(pl.multiple_of(i * CHUNK, CHUNK), CHUNK)
            total = self.staged[0, rows, :].astype(jnp.float32)
            for k in range(1, self.n):
                total = total + self.arrived[k, rows, :].astype(jnp.float32)
            self.out[rows, :] = total.astype(jnp.bfloat16)
            return carry

        lax.fori_loop(0, self.x.shape[1] // CHUNK, body, 0)
        for k in range(1, self.n):
            self.far(k).wait_send()
        for k in range(self.n):
            self.near(k).wait_send()


def gather_sems(n):
    return [DMA((n,)), DMA((n,)), DMA((n,)), DMA((n,)), DMA]


def scatter_scratch(count, shape):
    n = count // 2
    buffers = [pltpu.VMEM((n,) + shape, jnp.bfloat16) for unused in range(3)]
    return buffers + [DMA((n,)), DMA((n,)), DMA((n,)), DMA((n,))]


def params(number, mib=48):
    return pltpu.CompilerParams(
        collective_id=number, has_side_effects=True, vmem_limit_bytes=mib * 2**20
    )


def gather_kernel(count, x, out, *sems):
    greet(False, count, 0)
    work = Gather(count, x, out, *sems)
    work.start()
    work.forward()
    work.finish()


def gather_grad(count, out_grad):
    return pl.pallas_call(
        functools.partial(gather_kernel, count),
        out_shape=jax.ShapeDtypeStruct((count,) + out_grad.shape, out_grad.dtype),
        in_specs=[ANY],
        out_specs=ANY,
        scratch_shapes=gather_sems(count // 2),
        compiler_params=params(1, 16),
        name="gather_out_grad",
    )(out_grad)


def middle_kernel(count, fs, k_ref, v_ref, part_ref, k_out, v_out, head_out, *scratch):
    k_sems, v_sems = scratch[:5], scratch[5:10]
    parts, summed, z_send, z_recv, s_send, s_recv, local = scratch[10:]
    me = lax.axis_index("seq")
    mine = lax.axis_index("fsdp")
    greet(True, count, fs)

    def z_copy(k):
        other = lax.rem(mine + k, fs)
        return remote(part_ref.at[other], parts.at[k], z_send.at[k], z_recv.at[k], fsdp=other)

    def s_copy(k):
        other = lax.rem(me + k, count)
        return remote(summed.at[other], head_out.at[me], s_send.at[k], s_recv.at[k], seq=other)

    for k in range(1, fs):
        z_copy(k).start()
    works = [Gather(count, k_ref, k_out, *k_sems), Gather(count, v_ref, v_out, *v_sems)]
    for work in works:
        work.start()
    for k in range(1, fs):
        z_copy(k).wait_recv()

    def body(j, carry):
        total = part_ref[mine, j].astype(jnp.float32)
        for k in range(1, fs):
            total = total + parts[k, j].astype(jnp.float32)
        summed[j] = total.astype(jnp.bfloat16)
        return carry

    lax.fori_loop(0, count, body, 0)
    for k in range(1, count):
        s_copy(k).start()
    own = pltpu.make_async_copy(summed.at[me], head_out.at[me], local)
    own.start()
    for work in works:
        work.forward()
    for work in works:
        work.finish()
    own.wait()
    for k in range(1, fs):
        z_copy(k).wait_send()
    for k in range(1, count):
        s_copy(k).wait()


def middle(count, fs, key_rows, value_rows, part):
    slots = part.shape[1:]
    return pl.pallas_call(
        functools.partial(middle_kernel, count, fs),
        out_shape=[
            jax.ShapeDtypeStruct((count,) + key_rows.shape, jnp.bfloat16),
            jax.ShapeDtypeStruct((count,) + key_rows.shape, jnp.bfloat16),
            jax.ShapeDtypeStruct(slots, jnp.bfloat16),
        ],
        in_specs=[ANY, ANY, VMEM],
        out_specs=[ANY, ANY, ANY],
        scratch_shapes=gather_sems(count // 2)
        + gather_sems(count // 2)
        + [
            pltpu.VMEM((fs,) + slots, jnp.bfloat16),
            pltpu.VMEM(slots, jnp.bfloat16),
            DMA((fs,)),
            DMA((fs,)),
            DMA((count,)),
            DMA((count,)),
            DMA,
        ],
        compiler_params=params(2),
        name="gather_keys_values_sum_head_grad",
    )(key_rows, value_rows, part)


def attend_kernel(blocks, pat, q_ref, k_ref, v_ref, g_ref, att_ref, qg_ref, kg_ref, vg_ref, *scratch):
    k_set, v_set, k_acc, v_acc = scratch
    scale = 1.0 / math.sqrt(HD)
    f32, low = jnp.float32, jnp.bfloat16
    k_acc[...] = jnp.zeros_like(k_acc)
    v_acc[...] = jnp.zeros_like(v_acc)
    nt = (((1,), (1,)), ((), ()))
    nn = (((1,), (0,)), ((), ()))
    tn = (((0,), (0,)), ((), ()))

    def dot(a, b, dims):
        return lax.dot_general(a, b, dims, preferred_element_type=f32)

    for j in range(blocks):
        here = slice(j * BLK, (j + 1) * BLK)
        for s in range(NSEL):
            at = pl.ds(pl.multiple_of(pat[j, s] * BLK, BLK), BLK)
            k_set[s * BLK : (s + 1) * BLK, :] = k_ref[at, :]
            v_set[s * BLK : (s + 1) * BLK, :] = v_ref[at, :]
        q = q_ref[here, :]
        g = g_ref[:, here]
        scores = dot(k_set[...], q, nt) * scale
        top = jnp.max(scores, axis=0, keepdims=True)
        exps = jnp.exp(scores - top)
        probs = exps * (1.0 / jnp.sum(exps, axis=0, keepdims=True))
        probs_low = probs.astype(low)
        att_ref[:, here] = dot(v_set[...], probs_low, tn).astype(low)
        prob_grad = dot(v_set[...], g, nn)
        center = jnp.sum(probs * prob_grad, axis=0, keepdims=True)
        score_grad = (probs * (prob_grad - center)).astype(low)
        qg_ref[here, :] = (dot(score_grad, k_set[...], tn) * scale).astype(low)
        k_term = (dot(score_grad, q, nn) * scale).astype(low)
        v_term = dot(probs_low, g, nt).astype(low)
        for s in range(NSEL):
            at = pl.ds(pl.multiple_of(pat[j, s] * BLK, BLK), BLK)
            k_acc[at, :] += k_term[s * BLK : (s + 1) * BLK, :].astype(f32)
            v_acc[at, :] += v_term[s * BLK : (s + 1) * BLK, :].astype(f32)
    kg_ref[...] = k_acc[...].astype(low)
    vg_ref[...] = v_acc[...].astype(low)


def attend(pattern, queries, keys, values, grad_t):
    rows, width = queries.shape
    tokens = keys.shape[0]
    low = jnp.bfloat16
    by_col = lambda n: pl.BlockSpec((n, HD), lambda h, pat: (0, h))
    by_row = pl.BlockSpec((HD, rows), lambda h, pat: (h, 0))
    return pl.pallas_call(
        functools.partial(attend_kernel, rows // BLK),
        grid_spec=pltpu.PrefetchScalarGridSpec(
            num_scalar_prefetch=1,
            grid=(width // HD,),
            in_specs=[by_col(rows), by_col(tokens), by_col(tokens), by_row],
            out_specs=[by_row, by_col(rows), by_col(tokens), by_col(tokens)],
            scratch_shapes=[
                pltpu.VMEM((NSEL * BLK, HD), low),
                pltpu.VMEM((NSEL * BLK, HD), low),
                pltpu.VMEM((tokens, HD), jnp.float32),
                pltpu.VMEM((tokens, HD), jnp.float32),
            ],
        ),
        out_shape=[
            jax.ShapeDtypeStruct((width, rows), low),
            jax.ShapeDtypeStruct((rows, width), low),
            jax.ShapeDtypeStruct((tokens, width), low),
            jax.ShapeDtypeStruct((tokens, width), low),
        ],
        compiler_params=pltpu.CompilerParams(vmem_limit_bytes=48 * 2**20),
        name="attend",
    )(pattern, queries, keys, values, grad_t)


def late_kernel(count, fs, kg_ref, vg_ref, att_ref, k_out, v_out, att_out, *scratch):
    k_scratch, v_scratch = scratch[:7], scratch[7:14]
    s_send, s_recv, z_send, z_recv, local = scratch[14:]
    me = lax.axis_index("seq")
    mine = lax.axis_index("fsdp")
    greet(True, count, fs)

    def s_copy(k):
        other = lax.rem(me + k, count)
        return remote(
            att_ref.at[other], att_out.at[mine, me], s_send.at[k], s_recv.at[k], seq=other
        )

    def z_copy(k):
        other = lax.rem(mine + k, fs)
        return remote(att_out.at[mine], att_out.at[mine], z_send.at[k], z_recv.at[k], fsdp=other)

    for k in range(1, count):
        s_copy(k).start()
    own = pltpu.make_async_copy(att_ref.at[me], att_out.at[mine, me], local)
    own.start()
    works = [
        Scatter(count, kg_ref, k_out, *k_scratch),
        Scatter(count, vg_ref, v_out, *v_scratch),
    ]
    for work in works:
        work.start()
    own.wait()
    for k in range(1, count):
        s_copy(k).wait_recv()
    for k in range(1, fs):
        z_copy(k).start()
    for k in list(range(1, count // 2)) + [0]:
        for work in works:
            work.exchange(k)
    for work in works:
        work.finish()
    for k in range(1, count):
        s_copy(k).wait_send()
    for k in range(1, fs):
        z_copy(k).wait()


def late(count, fs, key_sums, value_sums, att):
    shape = key_sums.shape[1:]
    return pl.pallas_call(
        functools.partial(late_kernel, count, fs),
        out_shape=[
            jax.ShapeDtypeStruct(shape, jnp.bfloat16),
            jax.ShapeDtypeStruct(shape, jnp.bfloat16),
            jax.ShapeDtypeStruct((fs,) + att.shape, jnp.bfloat16),
        ],
        in_specs=[VMEM, VMEM, ANY],
        out_specs=[VMEM, VMEM, ANY],
        scratch_shapes=scatter_scratch(count, shape)
        + scatter_scratch(count, shape)
        + [DMA((count,)), DMA((count,)), DMA((fs,)), DMA((fs,)), DMA],
        compiler_params=params(3, 56),
        name="sum_key_value_grads_gather_attended",
    )(key_sums, value_sums, att)


def scatter_kernel(count, x, out, *scratch):
    greet(False, count, 0)
    work = Scatter(count, x, out, *scratch)
    work.start()
    for k in list(range(1, count // 2)) + [0]:
        work.exchange(k)
    work.finish()


def scatter_projected(count, partial):
    shape = partial.shape[1:]
    return pl.pallas_call(
        functools.partial(scatter_kernel, count),
        out_shape=jax.ShapeDtypeStruct(shape, jnp.bfloat16),
        in_specs=[VMEM],
        out_specs=VMEM,
        scratch_shapes=scatter_scratch(count, shape),
        compiler_params=params(4, 56),
        name="sum_projected",
    )(partial)


def shards(count, fs, queries, key_rows, value_rows, pattern, out_weight, out_grad):
    rows, width = queries.shape
    heads = width // HD
    part_e, heads_all, cols = out_weight.shape
    tokens = rows * count
    f32, low = jnp.float32, jnp.bfloat16
    weight = out_weight.reshape(part_e * heads_all, cols)

    grad_all = gather_grad(count, out_grad).reshape(tokens, cols)
    head_part = lax.dot_general(
        weight, grad_all, (((1,), (1,)), ((), ())), preferred_element_type=f32
    ).astype(low)
    head_part = head_part.reshape(part_e, fs, heads, count, rows)
    head_part = head_part.transpose(1, 3, 0, 2, 4).reshape(fs, count, part_e * heads, rows)

    keys, values, head_grad = middle(count, fs, key_rows, value_rows, head_part)
    grad_t = head_grad.reshape(count, part_e, heads, rows).transpose(2, 0, 1, 3)
    att_t, query_grad, key_sums, value_sums = attend(
        pattern,
        queries,
        keys.reshape(tokens, width),
        values.reshape(tokens, width),
        grad_t.reshape(width, rows),
    )
    att = att_t.reshape(heads, count, part_e, rows).transpose(1, 2, 0, 3)
    key_grad, value_grad, att_all = late(
        count,
        fs,
        key_sums.reshape(count, rows, width),
        value_sums.reshape(count, rows, width),
        att.reshape(count, part_e * heads, rows),
    )
    att_all = att_all.reshape(fs, count, part_e, heads, rows).transpose(2, 0, 3, 1, 4)
    att_all = att_all.reshape(part_e * heads_all, tokens)
    partial = lax.dot_general(
        att_all, weight, (((0,), (0,)), ((), ())), preferred_element_type=f32
    ).astype(low)
    projected = scatter_projected(count, partial.reshape(count, rows, cols))
    weight_grad = lax.dot_general(
        att_all, grad_all, (((1,), (0,)), ((), ())), preferred_element_type=f32
    ).reshape(part_e, heads_all, cols)
    return (projected, query_grad, key_grad, value_grad, weight_grad)


def solution(mesh):
    placed = (
        P("seq", "fsdp"),
        P("seq", "fsdp"),
        P("seq", "fsdp"),
        P("seq", None),
        P("seq", None, "fsdp"),
        P("seq", "fsdp"),
    )
    return jax.shard_map(
        functools.partial(shards, mesh.shape["seq"], mesh.shape["fsdp"]),
        mesh=mesh,
        in_specs=placed,
        out_specs=(
            P("seq", "fsdp"),
            P("seq", "fsdp"),
            P("seq", "fsdp"),
            P("seq", "fsdp"),
            P("seq", None, "fsdp"),
        ),
        check_vma=False,
    )
```

```python
import functools
import math

import jax
import jax.numpy as jnp
from jax import lax
from jax.experimental import pallas as pl
from jax.experimental.pallas import tpu as pltpu
from jax.sharding import PartitionSpec as P

HD = 128
BLK = 128
NSEL = 8
MESH = pl.DeviceIdType.MESH
ANY = pl.BlockSpec(memory_space=pl.ANY)
VMEM = pl.BlockSpec(memory_space=pltpu.VMEM)
DMA = pltpu.SemaphoreType.DMA
CHUNK = 32


def remote(src, dst, send_sem, recv_sem, **where):
    return pltpu.make_async_remote_copy(
        src_ref=src,
        dst_ref=dst,
        send_sem=send_sem,
        recv_sem=recv_sem,
        device_id=where,
        device_id_type=MESH,
    )


def chip_place():
    me = lax.axis_index("seq")
    core = lax.rem(me, 2)
    chip = me // 2
    return me, chip, core, chip * 2 + 1 - core


def greet(seq_all, count, fsdp_count):
    me, chip, core, partner = chip_place()
    barrier = pltpu.get_barrier_semaphore()
    total = 0
    if seq_all:
        for k in range(1, count):
            pl.semaphore_signal(
                barrier, inc=1, device_id={"seq": lax.rem(me + k, count)}, device_id_type=MESH
            )
            total += 1
    else:
        pl.semaphore_signal(barrier, inc=1, device_id={"seq": partner}, device_id_type=MESH)
        total += 1
        for k in range(1, count // 2):
            other = lax.rem(chip + k, count // 2) * 2 + core
            pl.semaphore_signal(barrier, inc=1, device_id={"seq": other}, device_id_type=MESH)
            total += 1
    if fsdp_count:
        mine = lax.axis_index("fsdp")
        for k in range(1, fsdp_count):
            other = lax.rem(mine + k, fsdp_count)
            pl.semaphore_signal(barrier, inc=1, device_id={"fsdp": other}, device_id_type=MESH)
            total += 1
    pl.semaphore_wait(barrier, total)


def chips(n):
    me, chip, core, partner = chip_place()
    if n != 4:
        there = [lax.rem(chip + k, n) for k in range(n)]
        return there, [lax.rem(chip + n - k, n) for k in range(n)]
    x, y = lax.rem(chip, 2), chip // 2
    beside, across = y * 2 + 1 - x, (1 - y) * 2 + x
    first = beside + core * (across - beside)
    second = across + core * (beside - across)
    return [chip, first, second, second], [chip, first, second, 3 - chip]


def mate(n, k):
    return 3 - k if n == 4 and k in (1, 2) else k


class Gather:
    def __init__(self, count, x, out, send, recv, near_send, near_recv, local):
        self.n = count // 2
        self.x, self.out = x, out
        self.send, self.recv = send, recv
        self.near_send, self.near_recv, self.local = near_send, near_recv, local
        self.me, self.chip, self.core, self.partner = chip_place()
        self.there, self.source = chips(self.n)

    def relayed(self, k):
        return self.n == 4 and k == 3

    def far(self, k):
        src, slot = self.x, self.me
        if self.relayed(k):
            slot = self.source[1] * 2 + self.core
            src = self.out.at[slot]
        other = self.there[k] * 2 + self.core
        return remote(src, self.out.at[slot], self.send.at[k], self.recv.at[k], seq=other)

    def near(self, k):
        slot = self.source[k] * 2 + self.core
        src = self.x if k == 0 else self.out.at[slot]
        return remote(
            src, self.out.at[slot], self.near_send.at[k], self.near_recv.at[k], seq=self.partner
        )

    def start(self):
        for k in range(1, self.n):
            if not self.relayed(k):
                self.far(k).start()
        self.near(0).start()
        self.own = pltpu.make_async_copy(self.x, self.out.at[self.me], self.local)
        self.own.start()

    def arrive(self, k):
        self.far(k).wait_recv()
        if k == 1 and self.n == 4:
            self.far(3).start()
        self.near(k).start()

    def finish_far(self):
        for k in range(1, self.n):
            self.far(k).wait_send()
        for k in range(self.n):
            self.near(k).wait_send()

    def finish(self):
        self.own.wait()
        self.finish_far()
        for k in range(self.n):
            self.near(k).wait_recv()


class Scatter:
    def __init__(self, count, x, out, got, staged, arrived, send, recv, near_send, near_recv):
        self.n = count // 2
        self.x, self.out, self.got, self.staged, self.arrived = x, out, got, staged, arrived
        self.send, self.recv, self.near_send, self.near_recv = send, recv, near_send, near_recv
        self.me, self.chip, self.core, self.partner = chip_place()
        self.there, self.source = chips(self.n)
        self.relay = self.n == 4
        self.dest = self.source if self.relay else self.there
        self.order = [3, 1, 2, 0] if self.relay else list(range(1, self.n)) + [0]

    def near_slot(self, k):
        return self.dest[mate(self.n, k)] * 2 + 1 - self.core

    def own_slot(self, k):
        return self.dest[k] * 2 + self.core

    def near(self, k):
        return remote(
            self.x.at[self.near_slot(k)],
            self.got.at[k],
            self.near_send.at[k],
            self.near_recv.at[k],
            seq=self.partner,
        )

    def far(self, k):
        chip = self.there[1] if self.relay and k == 3 else self.there[k]
        return remote(
            self.staged.at[k],
            self.arrived.at[k],
            self.send.at[k],
            self.recv.at[k],
            seq=chip * 2 + self.core,
        )

    def start(self):
        for k in self.order:
            self.near(k).start()

    def exchange(self, k):
        slot = self.own_slot(k)
        self.near(k).wait_recv()
        hop = self.relay and k == 2
        if hop:
            self.far(3).wait_recv()

        def body(i, carry):
            rows = pl.ds(pl.multiple_of(i * CHUNK, CHUNK), CHUNK)
            total = self.x[slot, rows, :].astype(jnp.float32) + self.got[k, rows, :].astype(
                jnp.float32
            )
            if hop:
                total = total + self.arrived[3, rows, :].astype(jnp.float32)
            self.staged[k, rows, :] = total.astype(jnp.bfloat16)
            return carry

        lax.fori_loop(0, self.x.shape[1] // CHUNK, body, 0)
        if k:
            self.far(k).start()

    def finish(self):
        last = [1, 2] if self.relay else list(range(1, self.n))
        for k in last:
            self.far(k).wait_recv()

        def body(i, carry):
            rows = pl.ds(pl.multiple_of(i * CHUNK, CHUNK), CHUNK)
            total = self.staged[0, rows, :].astype(jnp.float32)
            for k in last:
                total = total + self.arrived[k, rows, :].astype(jnp.float32)
            self.out[rows, :] = total.astype(jnp.bfloat16)
            return carry

        lax.fori_loop(0, self.x.shape[1] // CHUNK, body, 0)
        for k in range(1, self.n):
            self.far(k).wait_send()
        for k in range(self.n):
            self.near(k).wait_send()


def gather_sems(n):
    return [DMA((n,)), DMA((n,)), DMA((n,)), DMA((n,)), DMA]


def scatter_scratch(count, shape):
    n = count // 2
    buffers = [pltpu.VMEM((n,) + shape, jnp.bfloat16) for unused in range(3)]
    return buffers + [DMA((n,)), DMA((n,)), DMA((n,)), DMA((n,))]


def params(number, mib=48):
    return pltpu.CompilerParams(
        collective_id=number, has_side_effects=True, vmem_limit_bytes=mib * 2**20
    )


def first_kernel(count, fs, grad_ref, w_ref, k_ref, v_ref, grad_out, k_out, v_out, head_out, *scratch):
    n = count // 2
    grad = Gather(count, grad_ref, grad_out, *scratch[:5])
    works = [
        Gather(count, k_ref, k_out, *scratch[5:10]),
        Gather(count, v_ref, v_out, *scratch[10:15]),
    ]
    part, parts, summed, z_send, z_recv, s_send, s_recv, local = scratch[15:]
    me = lax.axis_index("seq")
    mine = lax.axis_index("fsdp")
    rows = w_ref.shape[0] // fs
    greet(True, count, fs)

    def z_copy(k, step):
        other = lax.rem(mine + k, fs)
        pair = pl.ds(grad.source[step] * 2, 2)
        at = k * n + step
        return remote(
            part.at[other, pair], parts.at[k, pair], z_send.at[at], z_recv.at[at], fsdp=other
        )

    def s_copy(k):
        other = lax.rem(me + k, count)
        return remote(summed.at[other], head_out.at[me], s_send.at[k], s_recv.at[k], seq=other)

    def multiply(step):
        for half in range(2):
            slot = grad.source[step] * 2 + half
            product = lax.dot_general(
                w_ref[...],
                grad_out[slot],
                (((1,), (1,)), ((), ())),
                preferred_element_type=jnp.float32,
            )
            for f in range(fs):
                part[f, slot] = product[f * rows : (f + 1) * rows].astype(jnp.bfloat16)
        for k in range(1, fs):
            z_copy(k, step).start()

    grad.start()
    grad.own.wait()
    grad.near(0).wait_recv()
    multiply(0)
    for k in range(1, n):
        grad.arrive(k)
        if k == n - 1:
            for work in works:
                work.start()
        if k > 1:
            grad.near(mate(n, k - 1)).wait_recv()
            multiply(k - 1)
    grad.near(n - 1).wait_recv()
    multiply(n - 1)
    for k in range(1, n - 1):
        for work in works:
            work.arrive(k)
    for k in range(1, fs):
        for step in range(n):
            z_copy(k, step).wait_recv()

    def body(j, carry):
        total = part[mine, j].astype(jnp.float32)
        for k in range(1, fs):
            total = total + parts[k, j].astype(jnp.float32)
        summed[j] = total.astype(jnp.bfloat16)
        return carry

    lax.fori_loop(0, count, body, 0)
    for k in range(1, count):
        s_copy(k).start()
    own = pltpu.make_async_copy(summed.at[me], head_out.at[me], local)
    own.start()
    grad.finish_far()
    for work in works:
        work.arrive(n - 1)
    for work in works:
        work.finish()
    own.wait()
    for k in range(1, fs):
        for step in range(n):
            z_copy(k, step).wait_send()
    for k in range(1, count):
        s_copy(k).wait()


def first(count, fs, out_grad, weight, key_rows, value_rows):
    n = count // 2
    low = jnp.bfloat16
    slots = (count, weight.shape[0] // fs, out_grad.shape[0])
    return pl.pallas_call(
        functools.partial(first_kernel, count, fs),
        out_shape=[
            jax.ShapeDtypeStruct((count,) + out_grad.shape, low),
            jax.ShapeDtypeStruct((count,) + key_rows.shape, low),
            jax.ShapeDtypeStruct((count,) + key_rows.shape, low),
            jax.ShapeDtypeStruct(slots, low),
        ],
        in_specs=[ANY, VMEM, ANY, ANY],
        out_specs=[VMEM, ANY, ANY, ANY],
        scratch_shapes=gather_sems(n)
        + gather_sems(n)
        + gather_sems(n)
        + [
            pltpu.VMEM((fs,) + slots, low),
            pltpu.VMEM((fs,) + slots, low),
            pltpu.VMEM(slots, low),
            DMA((fs * n,)),
            DMA((fs * n,)),
            DMA((count,)),
            DMA((count,)),
            DMA,
        ],
        compiler_params=params(1),
        name="gather_inputs_sum_head_grad",
    )(out_grad, weight, key_rows, value_rows)


def attend_kernel(blocks, pat, q_ref, k_ref, v_ref, g_ref, att_ref, qg_ref, kg_ref, vg_ref, *scratch):
    k_set, v_set, k_acc, v_acc = scratch
    scale = 1.0 / math.sqrt(HD)
    f32, low = jnp.float32, jnp.bfloat16
    k_acc[...] = jnp.zeros_like(k_acc)
    v_acc[...] = jnp.zeros_like(v_acc)
    nt = (((1,), (1,)), ((), ()))
    nn = (((1,), (0,)), ((), ()))
    tn = (((0,), (0,)), ((), ()))

    def dot(a, b, dims):
        return lax.dot_general(a, b, dims, preferred_element_type=f32)

    for j in range(blocks):
        here = slice(j * BLK, (j + 1) * BLK)
        for s in range(NSEL):
            at = pl.ds(pl.multiple_of(pat[j, s] * BLK, BLK), BLK)
            k_set[s * BLK : (s + 1) * BLK, :] = k_ref[at, :]
            v_set[s * BLK : (s + 1) * BLK, :] = v_ref[at, :]
        q = q_ref[here, :]
        g = g_ref[:, here]
        scores = dot(k_set[...], q, nt) * scale
        top = jnp.max(scores, axis=0, keepdims=True)
        exps = jnp.exp(scores - top)
        probs = exps * (1.0 / jnp.sum(exps, axis=0, keepdims=True))
        probs_low = probs.astype(low)
        att_ref[:, here] = dot(v_set[...], probs_low, tn).astype(low)
        prob_grad = dot(v_set[...], g, nn)
        center = jnp.sum(probs * prob_grad, axis=0, keepdims=True)
        score_grad = (probs * (prob_grad - center)).astype(low)
        qg_ref[here, :] = (dot(score_grad, k_set[...], tn) * scale).astype(low)
        k_term = (dot(score_grad, q, nn) * scale).astype(low)
        v_term = dot(probs_low, g, nt).astype(low)
        for s in range(NSEL):
            at = pl.ds(pl.multiple_of(pat[j, s] * BLK, BLK), BLK)
            k_acc[at, :] += k_term[s * BLK : (s + 1) * BLK, :].astype(f32)
            v_acc[at, :] += v_term[s * BLK : (s + 1) * BLK, :].astype(f32)
    kg_ref[...] = k_acc[...].astype(low)
    vg_ref[...] = v_acc[...].astype(low)


def attend(pattern, queries, keys, values, grad_t):
    rows, width = queries.shape
    tokens = keys.shape[0]
    low = jnp.bfloat16
    by_col = lambda n: pl.BlockSpec((n, HD), lambda h, pat: (0, h))
    by_row = pl.BlockSpec((HD, rows), lambda h, pat: (h, 0))
    return pl.pallas_call(
        functools.partial(attend_kernel, rows // BLK),
        grid_spec=pltpu.PrefetchScalarGridSpec(
            num_scalar_prefetch=1,
            grid=(width // HD,),
            in_specs=[by_col(rows), by_col(tokens), by_col(tokens), by_row],
            out_specs=[by_row, by_col(rows), by_col(tokens), by_col(tokens)],
            scratch_shapes=[
                pltpu.VMEM((NSEL * BLK, HD), low),
                pltpu.VMEM((NSEL * BLK, HD), low),
                pltpu.VMEM((tokens, HD), jnp.float32),
                pltpu.VMEM((tokens, HD), jnp.float32),
            ],
        ),
        out_shape=[
            jax.ShapeDtypeStruct((width, rows), low),
            jax.ShapeDtypeStruct((rows, width), low),
            jax.ShapeDtypeStruct((tokens, width), low),
            jax.ShapeDtypeStruct((tokens, width), low),
        ],
        compiler_params=pltpu.CompilerParams(vmem_limit_bytes=48 * 2**20),
        name="attend",
    )(pattern, queries, keys, values, grad_t)


def late_kernel(count, fs, kg_ref, vg_ref, att_ref, k_out, v_out, att_out, *scratch):
    k_scratch, v_scratch = scratch[:7], scratch[7:14]
    s_send, s_recv, z_send, z_recv, local = scratch[14:]
    me = lax.axis_index("seq")
    mine = lax.axis_index("fsdp")
    greet(True, count, fs)

    def s_copy(k):
        other = lax.rem(me + k, count)
        return remote(
            att_ref.at[other], att_out.at[mine, me], s_send.at[k], s_recv.at[k], seq=other
        )

    def z_copy(k):
        other = lax.rem(mine + k, fs)
        return remote(att_out.at[mine], att_out.at[mine], z_send.at[k], z_recv.at[k], fsdp=other)

    for k in range(1, count):
        s_copy(k).start()
    own = pltpu.make_async_copy(att_ref.at[me], att_out.at[mine, me], local)
    own.start()
    works = [
        Scatter(count, kg_ref, k_out, *k_scratch),
        Scatter(count, vg_ref, v_out, *v_scratch),
    ]
    for work in works:
        work.start()
    own.wait()
    for k in range(1, count):
        s_copy(k).wait_recv()
    for k in range(1, fs):
        z_copy(k).start()
    for k in works[0].order:
        for work in works:
            work.exchange(k)
    for work in works:
        work.finish()
    for k in range(1, count):
        s_copy(k).wait_send()
    for k in range(1, fs):
        z_copy(k).wait()


def late(count, fs, key_sums, value_sums, att):
    shape = key_sums.shape[1:]
    return pl.pallas_call(
        functools.partial(late_kernel, count, fs),
        out_shape=[
            jax.ShapeDtypeStruct(shape, jnp.bfloat16),
            jax.ShapeDtypeStruct(shape, jnp.bfloat16),
            jax.ShapeDtypeStruct((fs,) + att.shape, jnp.bfloat16),
        ],
        in_specs=[VMEM, VMEM, ANY],
        out_specs=[VMEM, VMEM, ANY],
        scratch_shapes=scatter_scratch(count, shape)
        + scatter_scratch(count, shape)
        + [DMA((count,)), DMA((count,)), DMA((fs,)), DMA((fs,)), DMA],
        compiler_params=params(3, 56),
        name="sum_key_value_grads_gather_attended",
    )(key_sums, value_sums, att)


def last_kernel(count, att_ref, w_ref, grad_ref, out, weight_out, partial, *scratch):
    greet(False, count, 0)
    work = Scatter(count, partial, out, *scratch)
    rows = out.shape[0]

    def multiply(slot):
        cols = pl.ds(pl.multiple_of(slot * rows, rows), rows)
        partial[slot] = lax.dot_general(
            att_ref[:, cols],
            w_ref[...],
            (((0,), (0,)), ((), ())),
            preferred_element_type=jnp.float32,
        ).astype(jnp.bfloat16)

    for k in work.order:
        multiply(work.near_slot(k))
        work.near(k).start()
    for k in work.order:
        multiply(work.own_slot(k))
        if k:
            work.exchange(k)

    def columns(i, carry):
        cols = pl.ds(pl.multiple_of(i * 256, 256), 256)
        weight_out[:, cols] = jnp.dot(
            att_ref[...], grad_ref[:, cols], preferred_element_type=jnp.float32
        )
        return carry

    lax.fori_loop(0, w_ref.shape[1] // 256, columns, 0)
    work.exchange(0)
    work.finish()


def last(count, att_all, weight, grad_all):
    rows = grad_all.shape[0] // count
    shape = (rows, grad_all.shape[1])
    return pl.pallas_call(
        functools.partial(last_kernel, count),
        out_shape=[
            jax.ShapeDtypeStruct(shape, jnp.bfloat16),
            jax.ShapeDtypeStruct(weight.shape, jnp.float32),
        ],
        in_specs=[VMEM, VMEM, VMEM],
        out_specs=[VMEM, VMEM],
        scratch_shapes=[pltpu.VMEM((count,) + shape, jnp.bfloat16)] + scatter_scratch(count, shape),
        compiler_params=params(4, 56),
        name="project_sum_weight_grad",
    )(att_all, weight, grad_all)


def shards(count, fs, queries, key_rows, value_rows, pattern, out_weight, out_grad):
    rows, width = queries.shape
    heads = width // HD
    part_e, heads_all, cols = out_weight.shape
    tokens = rows * count
    weight = out_weight.transpose(1, 0, 2).reshape(heads_all * part_e, cols)

    grad_all, keys, values, head_grad = first(count, fs, out_grad, weight, key_rows, value_rows)
    grad_t = head_grad.reshape(count, heads, part_e, rows).transpose(1, 0, 2, 3)
    att_t, query_grad, key_sums, value_sums = attend(
        pattern,
        queries,
        keys.reshape(tokens, width),
        values.reshape(tokens, width),
        grad_t.reshape(width, rows),
    )
    att = att_t.reshape(heads, count, part_e, rows).transpose(1, 0, 2, 3)
    key_grad, value_grad, att_all = late(
        count,
        fs,
        key_sums.reshape(count, rows, width),
        value_sums.reshape(count, rows, width),
        att.reshape(count, heads * part_e, rows),
    )
    att_all = att_all.transpose(0, 2, 1, 3).reshape(heads_all * part_e, tokens)
    projected, weight_grad = last(count, att_all, weight, grad_all.reshape(tokens, cols))
    weight_grad = weight_grad.reshape(heads_all, part_e, cols).transpose(1, 0, 2)
    return (projected, query_grad, key_grad, value_grad, weight_grad)


def solution(mesh):
    placed = (
        P("seq", "fsdp"),
        P("seq", "fsdp"),
        P("seq", "fsdp"),
        P("seq", None),
        P("seq", None, "fsdp"),
        P("seq", "fsdp"),
    )
    return jax.shard_map(
        functools.partial(shards, mesh.shape["seq"], mesh.shape["fsdp"]),
        mesh=mesh,
        in_specs=placed,
        out_specs=(
            P("seq", "fsdp"),
            P("seq", "fsdp"),
            P("seq", "fsdp"),
            P("seq", "fsdp"),
            P("seq", None, "fsdp"),
        ),
        check_vma=False,
    )
```

```python
import functools
import math

import jax
import jax.numpy as jnp
from jax import lax
from jax.experimental import pallas as pl
from jax.experimental.pallas import tpu as pltpu
from jax.sharding import PartitionSpec as P

HD = 128
BLK = 128
NSEL = 8
MESH = pl.DeviceIdType.MESH
ANY = pl.BlockSpec(memory_space=pl.ANY)
VMEM = pl.BlockSpec(memory_space=pltpu.VMEM)
DMA = pltpu.SemaphoreType.DMA
CHUNK = 32


def remote(src, dst, send_sem, recv_sem, **where):
    return pltpu.make_async_remote_copy(
        src_ref=src,
        dst_ref=dst,
        send_sem=send_sem,
        recv_sem=recv_sem,
        device_id=where,
        device_id_type=MESH,
    )


def chip_place():
    me = lax.axis_index("seq")
    core = lax.rem(me, 2)
    chip = me // 2
    return me, chip, core, chip * 2 + 1 - core


def greet(seq_all, count, fsdp_count):
    me, chip, core, partner = chip_place()
    barrier = pltpu.get_barrier_semaphore()
    total = 0
    if seq_all:
        for k in range(1, count):
            pl.semaphore_signal(
                barrier, inc=1, device_id={"seq": lax.rem(me + k, count)}, device_id_type=MESH
            )
            total += 1
    else:
        pl.semaphore_signal(barrier, inc=1, device_id={"seq": partner}, device_id_type=MESH)
        total += 1
        for k in range(1, count // 2):
            other = lax.rem(chip + k, count // 2) * 2 + core
            pl.semaphore_signal(barrier, inc=1, device_id={"seq": other}, device_id_type=MESH)
            total += 1
    if fsdp_count:
        mine = lax.axis_index("fsdp")
        for k in range(1, fsdp_count):
            other = lax.rem(mine + k, fsdp_count)
            pl.semaphore_signal(barrier, inc=1, device_id={"fsdp": other}, device_id_type=MESH)
            total += 1
    pl.semaphore_wait(barrier, total)


def chips(n):
    me, chip, core, partner = chip_place()
    if n != 4:
        there = [lax.rem(chip + k, n) for k in range(n)]
        return there, [lax.rem(chip + n - k, n) for k in range(n)]
    x, y = lax.rem(chip, 2), chip // 2
    beside, across = y * 2 + 1 - x, (1 - y) * 2 + x
    first = beside + core * (across - beside)
    second = across + core * (beside - across)
    return [chip, first, second, second], [chip, first, second, 3 - chip]


def mate(n, k):
    return 3 - k if n == 4 and k in (1, 2) else k


class Gather:
    def __init__(self, count, x, out, send, recv, near_send, near_recv, local):
        self.n = count // 2
        self.x, self.out = x, out
        self.send, self.recv = send, recv
        self.near_send, self.near_recv, self.local = near_send, near_recv, local
        self.me, self.chip, self.core, self.partner = chip_place()
        self.there, self.source = chips(self.n)

    def relayed(self, k):
        return self.n == 4 and k == 3

    def far(self, k):
        src, slot = self.x, self.me
        if self.relayed(k):
            slot = self.source[1] * 2 + self.core
            src = self.out.at[slot]
        other = self.there[k] * 2 + self.core
        return remote(src, self.out.at[slot], self.send.at[k], self.recv.at[k], seq=other)

    def near(self, k):
        slot = self.source[k] * 2 + self.core
        src = self.x if k == 0 else self.out.at[slot]
        return remote(
            src, self.out.at[slot], self.near_send.at[k], self.near_recv.at[k], seq=self.partner
        )

    def start(self):
        for k in range(1, self.n):
            if not self.relayed(k):
                self.far(k).start()
        self.near(0).start()
        self.own = pltpu.make_async_copy(self.x, self.out.at[self.me], self.local)
        self.own.start()

    def arrive(self, k):
        self.far(k).wait_recv()
        if k == 1 and self.n == 4:
            self.far(3).start()
        self.near(k).start()

    def finish_far(self):
        for k in range(1, self.n):
            self.far(k).wait_send()
        for k in range(self.n):
            self.near(k).wait_send()

    def finish(self):
        self.own.wait()
        self.finish_far()
        for k in range(self.n):
            self.near(k).wait_recv()


class Scatter:
    def __init__(self, count, x, out, got, staged, arrived, send, recv, near_send, near_recv):
        self.n = count // 2
        self.x, self.out, self.got, self.staged, self.arrived = x, out, got, staged, arrived
        self.send, self.recv, self.near_send, self.near_recv = send, recv, near_send, near_recv
        self.me, self.chip, self.core, self.partner = chip_place()
        self.there, self.source = chips(self.n)
        self.relay = self.n == 4
        self.dest = self.source if self.relay else self.there
        self.order = [3, 1, 2, 0] if self.relay else list(range(1, self.n)) + [0]

    def near_slot(self, k):
        return self.dest[mate(self.n, k)] * 2 + 1 - self.core

    def own_slot(self, k):
        return self.dest[k] * 2 + self.core

    def near(self, k):
        return remote(
            self.x.at[self.near_slot(k)],
            self.got.at[k],
            self.near_send.at[k],
            self.near_recv.at[k],
            seq=self.partner,
        )

    def far(self, k):
        chip = self.there[1] if self.relay and k == 3 else self.there[k]
        return remote(
            self.staged.at[k],
            self.arrived.at[k],
            self.send.at[k],
            self.recv.at[k],
            seq=chip * 2 + self.core,
        )

    def start(self):
        for k in self.order:
            self.near(k).start()

    def exchange(self, k):
        slot = self.own_slot(k)
        self.near(k).wait_recv()
        hop = self.relay and k == 2
        if hop:
            self.far(3).wait_recv()

        def body(i, carry):
            rows = pl.ds(pl.multiple_of(i * CHUNK, CHUNK), CHUNK)
            total = self.x[slot, rows, :].astype(jnp.float32) + self.got[k, rows, :].astype(
                jnp.float32
            )
            if hop:
                total = total + self.arrived[3, rows, :].astype(jnp.float32)
            self.staged[k, rows, :] = total.astype(jnp.bfloat16)
            return carry

        lax.fori_loop(0, self.x.shape[1] // CHUNK, body, 0)
        if k:
            self.far(k).start()

    def finish(self):
        last = [1, 2] if self.relay else list(range(1, self.n))
        for k in last:
            self.far(k).wait_recv()

        def body(i, carry):
            rows = pl.ds(pl.multiple_of(i * CHUNK, CHUNK), CHUNK)
            total = self.staged[0, rows, :].astype(jnp.float32)
            for k in last:
                total = total + self.arrived[k, rows, :].astype(jnp.float32)
            self.out[rows, :] = total.astype(jnp.bfloat16)
            return carry

        lax.fori_loop(0, self.x.shape[1] // CHUNK, body, 0)
        for k in range(1, self.n):
            self.far(k).wait_send()
        for k in range(self.n):
            self.near(k).wait_send()


def gather_sems(n):
    return [DMA((n,)), DMA((n,)), DMA((n,)), DMA((n,)), DMA]


def scatter_scratch(count, shape):
    n = count // 2
    buffers = [pltpu.VMEM((n,) + shape, jnp.bfloat16) for unused in range(3)]
    return buffers + [DMA((n,)), DMA((n,)), DMA((n,)), DMA((n,))]


def params(number, mib=48):
    return pltpu.CompilerParams(
        collective_id=number, has_side_effects=True, vmem_limit_bytes=mib * 2**20
    )


def first_kernel(count, fs, grad_ref, w_ref, k_ref, v_ref, grad_out, k_out, v_out, head_out, *scratch):
    n = count // 2
    grad = Gather(count, grad_ref, grad_out, *scratch[:5])
    works = [
        Gather(count, k_ref, k_out, *scratch[5:10]),
        Gather(count, v_ref, v_out, *scratch[10:15]),
    ]
    part, parts, summed, z_send, z_recv, s_send, s_recv, local = scratch[15:]
    me = lax.axis_index("seq")
    mine = lax.axis_index("fsdp")
    rows = w_ref.shape[0] // fs
    greet(True, count, fs)

    def z_copy(k, step):
        other = lax.rem(mine + k, fs)
        pair = pl.ds(grad.source[step] * 2, 2)
        at = k * n + step
        return remote(
            part.at[other, pair], parts.at[k, pair], z_send.at[at], z_recv.at[at], fsdp=other
        )

    def s_copy(k):
        other = lax.rem(me + k, count)
        return remote(summed.at[other], head_out.at[me], s_send.at[k], s_recv.at[k], seq=other)

    def multiply(step):
        for half in range(2):
            slot = grad.source[step] * 2 + half
            product = lax.dot_general(
                w_ref[...],
                grad_out[slot],
                (((1,), (1,)), ((), ())),
                preferred_element_type=jnp.float32,
            )
            for f in range(fs):
                part[f, slot] = product[f * rows : (f + 1) * rows].astype(jnp.bfloat16)
        for k in range(1, fs):
            z_copy(k, step).start()

    grad.start()
    grad.own.wait()
    grad.near(0).wait_recv()
    multiply(0)
    for k in range(1, n):
        grad.arrive(k)
        if k == n - 1:
            for work in works:
                work.start()
        if k > 1:
            grad.near(mate(n, k - 1)).wait_recv()
            multiply(k - 1)
    grad.near(n - 1).wait_recv()
    multiply(n - 1)
    for k in range(1, n - 1):
        for work in works:
            work.arrive(k)
    for k in range(1, fs):
        for step in range(n):
            z_copy(k, step).wait_recv()

    def body(j, carry):
        total = part[mine, j].astype(jnp.float32)
        for k in range(1, fs):
            total = total + parts[k, j].astype(jnp.float32)
        summed[j] = total.astype(jnp.bfloat16)
        return carry

    lax.fori_loop(0, count, body, 0)
    for k in range(1, count):
        s_copy(k).start()
    own = pltpu.make_async_copy(summed.at[me], head_out.at[me], local)
    own.start()
    grad.finish_far()
    for work in works:
        work.arrive(n - 1)
    for work in works:
        work.finish()
    own.wait()
    for k in range(1, fs):
        for step in range(n):
            z_copy(k, step).wait_send()
    for k in range(1, count):
        s_copy(k).wait()


def first(count, fs, out_grad, weight, key_rows, value_rows):
    n = count // 2
    low = jnp.bfloat16
    slots = (count, weight.shape[0] // fs, out_grad.shape[0])
    return pl.pallas_call(
        functools.partial(first_kernel, count, fs),
        out_shape=[
            jax.ShapeDtypeStruct((count,) + out_grad.shape, low),
            jax.ShapeDtypeStruct((count,) + key_rows.shape, low),
            jax.ShapeDtypeStruct((count,) + key_rows.shape, low),
            jax.ShapeDtypeStruct(slots, low),
        ],
        in_specs=[ANY, VMEM, ANY, ANY],
        out_specs=[VMEM, ANY, ANY, ANY],
        scratch_shapes=gather_sems(n)
        + gather_sems(n)
        + gather_sems(n)
        + [
            pltpu.VMEM((fs,) + slots, low),
            pltpu.VMEM((fs,) + slots, low),
            pltpu.VMEM(slots, low),
            DMA((fs * n,)),
            DMA((fs * n,)),
            DMA((count,)),
            DMA((count,)),
            DMA,
        ],
        compiler_params=params(1),
        name="gather_inputs_sum_head_grad",
    )(out_grad, weight, key_rows, value_rows)


def attend_kernel(blocks, pat, q_ref, k_ref, v_ref, g_ref, att_ref, qg_ref, kg_ref, vg_ref, *scratch):
    k_set, v_set, k_acc, v_acc = scratch
    scale = 1.0 / math.sqrt(HD)
    f32, low = jnp.float32, jnp.bfloat16
    k_acc[...] = jnp.zeros_like(k_acc)
    v_acc[...] = jnp.zeros_like(v_acc)
    nt = (((1,), (1,)), ((), ()))
    nn = (((1,), (0,)), ((), ()))
    tn = (((0,), (0,)), ((), ()))

    def dot(a, b, dims):
        return lax.dot_general(a, b, dims, preferred_element_type=f32)

    for j in range(blocks):
        here = slice(j * BLK, (j + 1) * BLK)
        for s in range(NSEL):
            at = pl.ds(pl.multiple_of(pat[j, s] * BLK, BLK), BLK)
            k_set[s * BLK : (s + 1) * BLK, :] = k_ref[at, :]
            v_set[s * BLK : (s + 1) * BLK, :] = v_ref[at, :]
        q = q_ref[here, :]
        g = g_ref[:, here]
        scores = dot(k_set[...], q, nt) * scale
        top = jnp.max(scores, axis=0, keepdims=True)
        exps = jnp.exp(scores - top)
        probs = exps * (1.0 / jnp.sum(exps, axis=0, keepdims=True))
        probs_low = probs.astype(low)
        att_ref[:, here] = dot(v_set[...], probs_low, tn).astype(low)
        prob_grad = dot(v_set[...], g, nn)
        center = jnp.sum(probs * prob_grad, axis=0, keepdims=True)
        score_grad = (probs * (prob_grad - center)).astype(low)
        qg_ref[here, :] = (dot(score_grad, k_set[...], tn) * scale).astype(low)
        k_term = (dot(score_grad, q, nn) * scale).astype(low)
        v_term = dot(probs_low, g, nt).astype(low)
        for s in range(NSEL):
            at = pl.ds(pl.multiple_of(pat[j, s] * BLK, BLK), BLK)
            k_acc[at, :] += k_term[s * BLK : (s + 1) * BLK, :].astype(f32)
            v_acc[at, :] += v_term[s * BLK : (s + 1) * BLK, :].astype(f32)
    kg_ref[...] = k_acc[...].astype(low)
    vg_ref[...] = v_acc[...].astype(low)


def attend(pattern, queries, keys, values, grad_t):
    rows, width = queries.shape
    tokens = keys.shape[0]
    low = jnp.bfloat16
    by_col = lambda n: pl.BlockSpec((n, HD), lambda h, pat: (0, h))
    by_row = pl.BlockSpec((HD, rows), lambda h, pat: (h, 0))
    return pl.pallas_call(
        functools.partial(attend_kernel, rows // BLK),
        grid_spec=pltpu.PrefetchScalarGridSpec(
            num_scalar_prefetch=1,
            grid=(width // HD,),
            in_specs=[by_col(rows), by_col(tokens), by_col(tokens), by_row],
            out_specs=[by_row, by_col(rows), by_col(tokens), by_col(tokens)],
            scratch_shapes=[
                pltpu.VMEM((NSEL * BLK, HD), low),
                pltpu.VMEM((NSEL * BLK, HD), low),
                pltpu.VMEM((tokens, HD), jnp.float32),
                pltpu.VMEM((tokens, HD), jnp.float32),
            ],
        ),
        out_shape=[
            jax.ShapeDtypeStruct((width, rows), low),
            jax.ShapeDtypeStruct((rows, width), low),
            jax.ShapeDtypeStruct((tokens, width), low),
            jax.ShapeDtypeStruct((tokens, width), low),
        ],
        compiler_params=pltpu.CompilerParams(vmem_limit_bytes=48 * 2**20),
        name="attend",
    )(pattern, queries, keys, values, grad_t)


class Line:
    def __init__(self, fs, out, up_send, up_recv, down_send, down_recv):
        self.fs, self.out = fs, out
        self.up_sems, self.down_sems = (up_send, up_recv), (down_send, down_recv)
        self.mine = lax.axis_index("fsdp")

    def copy(self, sems, shard, step, other):
        slot = self.out.at[shard]
        return remote(slot, slot, sems[0].at[step], sems[1].at[step], fsdp=other)

    def sends(self, step, act):
        mine, end = self.mine, self.fs - 1

        @pl.when((mine >= step) & (mine < end))
        def up():
            act(self.copy(self.up_sems, mine - step, step, mine + 1))

        @pl.when((mine + step <= end) & (mine > 0))
        def down():
            act(self.copy(self.down_sems, mine + step, step, mine - 1))

    def start(self, step):
        self.sends(step, lambda copy: copy.start())

    def arrive(self, step):
        mine, end = self.mine, self.fs - 1

        @pl.when(mine - 1 >= step)
        def below():
            self.copy(self.up_sems, mine - 1 - step, step, mine - 1).wait_recv()

        @pl.when(mine + 1 + step <= end)
        def above():
            self.copy(self.down_sems, mine + 1 + step, step, mine + 1).wait_recv()

    def finish(self):
        for step in range(self.fs - 1):
            self.sends(step, lambda copy: copy.wait_send())


def late_kernel(count, fs, kg_ref, vg_ref, att_ref, k_out, v_out, att_out, *scratch):
    s_send, s_recv, local = scratch[14:17]
    line = Line(fs, att_out, *scratch[17:])
    me = lax.axis_index("seq")
    mine = lax.axis_index("fsdp")
    greet(True, count, fs)

    def s_copy(k):
        other = lax.rem(me + k, count)
        return remote(
            att_ref.at[other], att_out.at[mine, me], s_send.at[k], s_recv.at[k], seq=other
        )

    for k in range(1, count):
        s_copy(k).start()
    own = pltpu.make_async_copy(att_ref.at[me], att_out.at[mine, me], local)
    own.start()
    works = [
        Scatter(count, kg_ref, k_out, *scratch[:7]),
        Scatter(count, vg_ref, v_out, *scratch[7:14]),
    ]
    for work in works:
        work.start()
    order = works[0].order
    for work in works:
        work.exchange(order[0])
    own.wait()
    for k in range(1, count):
        s_copy(k).wait_recv()
    line.start(0)
    for i in range(1, max(len(order), fs)):
        if i < len(order):
            for work in works:
                work.exchange(order[i])
        if i < fs:
            line.arrive(i - 1)
            if i < fs - 1:
                line.start(i)
    for work in works:
        work.finish()
    for k in range(1, count):
        s_copy(k).wait_send()
    line.finish()


def late(count, fs, key_sums, value_sums, att):
    shape = key_sums.shape[1:]
    return pl.pallas_call(
        functools.partial(late_kernel, count, fs),
        out_shape=[
            jax.ShapeDtypeStruct(shape, jnp.bfloat16),
            jax.ShapeDtypeStruct(shape, jnp.bfloat16),
            jax.ShapeDtypeStruct((fs,) + att.shape, jnp.bfloat16),
        ],
        in_specs=[VMEM, VMEM, ANY],
        out_specs=[VMEM, VMEM, ANY],
        scratch_shapes=scatter_scratch(count, shape)
        + scatter_scratch(count, shape)
        + [DMA((count,)), DMA((count,)), DMA]
        + [DMA((fs,)) for unused in range(4)],
        compiler_params=params(3, 56),
        name="sum_key_value_grads_gather_attended",
    )(key_sums, value_sums, att)


def last_kernel(count, fs, part_e, att_ref, w_ref, grad_ref, out, weight_out, partial, flat, *scratch):
    greet(False, count, 0)
    work = Scatter(count, partial, out, *scratch)
    rows = out.shape[0]

    def multiply(slot):
        total = None
        for f in range(fs):
            term = lax.dot_general(
                att_ref[f, slot],
                w_ref[f],
                (((0,), (0,)), ((), ())),
                preferred_element_type=jnp.float32,
            )
            total = term if total is None else total + term
        partial[slot] = total.astype(jnp.bfloat16)

    for k in work.order:
        multiply(work.near_slot(k))
        work.near(k).start()
    for k in work.order:
        multiply(work.own_slot(k))
        if k:
            work.exchange(k)

    def flatten(j, carry):
        at = pl.ds(pl.multiple_of(j * rows, rows), rows)
        for f in range(fs):
            flat[f, :, at] = att_ref[f, j]
        return carry

    lax.fori_loop(0, count, flatten, 0)

    def columns(i, carry):
        cols = pl.ds(pl.multiple_of(i * 256, 256), 256)
        for f in range(fs):
            product = jnp.dot(flat[f], grad_ref[:, cols], preferred_element_type=jnp.float32)
            if part_e % 8:
                weight_out[f, :, cols] = product
                continue
            heads = product.shape[0] // part_e
            for h in range(heads):
                weight_out[:, f * heads + h, cols] = product[h * part_e : (h + 1) * part_e]
        return carry

    lax.fori_loop(0, w_ref.shape[2] // 256, columns, 0)
    work.exchange(0)
    work.finish()


def last(count, part_e, att_all, weight, grad_all):
    fs, rows_here, cols = weight.shape
    tokens = grad_all.shape[0]
    shape = (tokens // count, cols)
    heads_all = fs * rows_here // part_e
    by_position = part_e % 8 == 0
    grad_shape = (part_e, heads_all, cols) if by_position else weight.shape
    projected, weight_grad = pl.pallas_call(
        functools.partial(last_kernel, count, fs, part_e),
        out_shape=[
            jax.ShapeDtypeStruct(shape, jnp.bfloat16),
            jax.ShapeDtypeStruct(grad_shape, jnp.float32),
        ],
        in_specs=[VMEM, VMEM, VMEM],
        out_specs=[VMEM, VMEM],
        scratch_shapes=[
            pltpu.VMEM((count,) + shape, jnp.bfloat16),
            pltpu.VMEM((fs, rows_here, tokens), jnp.bfloat16),
        ]
        + scatter_scratch(count, shape),
        compiler_params=params(4, 56),
        name="project_sum_weight_grad",
    )(att_all, weight, grad_all)
    if not by_position:
        weight_grad = weight_grad.reshape(heads_all, part_e, cols).transpose(1, 0, 2)
    return projected, weight_grad


def shards(count, fs, queries, key_rows, value_rows, pattern, out_weight, out_grad):
    rows, width = queries.shape
    heads = width // HD
    part_e, heads_all, cols = out_weight.shape
    tokens = rows * count
    weight = out_weight.transpose(1, 0, 2).reshape(heads_all * part_e, cols)

    grad_all, keys, values, head_grad = first(count, fs, out_grad, weight, key_rows, value_rows)
    grad_t = head_grad.reshape(count, heads, part_e, rows).transpose(1, 0, 2, 3)
    att_t, query_grad, key_sums, value_sums = attend(
        pattern,
        queries,
        keys.reshape(tokens, width),
        values.reshape(tokens, width),
        grad_t.reshape(width, rows),
    )
    att = att_t.reshape(heads, count, part_e, rows).transpose(1, 0, 2, 3)
    key_grad, value_grad, att_all = late(
        count,
        fs,
        key_sums.reshape(count, rows, width),
        value_sums.reshape(count, rows, width),
        att.reshape(count, heads * part_e, rows),
    )
    projected, weight_grad = last(
        count,
        part_e,
        att_all,
        weight.reshape(fs, heads * part_e, cols),
        grad_all.reshape(tokens, cols),
    )
    return (projected, query_grad, key_grad, value_grad, weight_grad)


def solution(mesh):
    placed = (
        P("seq", "fsdp"),
        P("seq", "fsdp"),
        P("seq", "fsdp"),
        P("seq", None),
        P("seq", None, "fsdp"),
        P("seq", "fsdp"),
    )
    return jax.shard_map(
        functools.partial(shards, mesh.shape["seq"], mesh.shape["fsdp"]),
        mesh=mesh,
        in_specs=placed,
        out_specs=(
            P("seq", "fsdp"),
            P("seq", "fsdp"),
            P("seq", "fsdp"),
            P("seq", "fsdp"),
            P("seq", None, "fsdp"),
        ),
        check_vma=False,
    )
```

```python
import functools
import math

import jax
import jax.numpy as jnp
from jax import lax
from jax.experimental import pallas as pl
from jax.experimental.pallas import tpu as pltpu
from jax.sharding import PartitionSpec as P

HD = 128
BLK = 128
NSEL = 8
MESH = pl.DeviceIdType.MESH
ANY = pl.BlockSpec(memory_space=pl.ANY)
VMEM = pl.BlockSpec(memory_space=pltpu.VMEM)
DMA = pltpu.SemaphoreType.DMA
CHUNK = 32


def remote(src, dst, send_sem, recv_sem, **where):
    return pltpu.make_async_remote_copy(
        src_ref=src,
        dst_ref=dst,
        send_sem=send_sem,
        recv_sem=recv_sem,
        device_id=where,
        device_id_type=MESH,
    )


def chip_place():
    me = lax.axis_index("seq")
    core = lax.rem(me, 2)
    chip = me // 2
    return me, chip, core, chip * 2 + 1 - core


def greet(seq_all, count, fsdp_count):
    me, chip, core, partner = chip_place()
    barrier = pltpu.get_barrier_semaphore()
    total = 0
    if seq_all:
        for k in range(1, count):
            pl.semaphore_signal(
                barrier, inc=1, device_id={"seq": lax.rem(me + k, count)}, device_id_type=MESH
            )
            total += 1
    else:
        pl.semaphore_signal(barrier, inc=1, device_id={"seq": partner}, device_id_type=MESH)
        total += 1
        for k in range(1, count // 2):
            other = lax.rem(chip + k, count // 2) * 2 + core
            pl.semaphore_signal(barrier, inc=1, device_id={"seq": other}, device_id_type=MESH)
            total += 1
    if fsdp_count:
        mine = lax.axis_index("fsdp")
        for k in range(1, fsdp_count):
            other = lax.rem(mine + k, fsdp_count)
            pl.semaphore_signal(barrier, inc=1, device_id={"fsdp": other}, device_id_type=MESH)
            total += 1
    pl.semaphore_wait(barrier, total)


def chips(n):
    me, chip, core, partner = chip_place()
    if n != 4:
        there = [lax.rem(chip + k, n) for k in range(n)]
        return there, [lax.rem(chip + n - k, n) for k in range(n)]
    x, y = lax.rem(chip, 2), chip // 2
    beside, across = y * 2 + 1 - x, (1 - y) * 2 + x
    first = beside + core * (across - beside)
    second = across + core * (beside - across)
    return [chip, first, second, second], [chip, first, second, 3 - chip]


def mate(n, k):
    return 3 - k if n == 4 and k in (1, 2) else k


class Gather:
    def __init__(self, count, x, out, send, recv, near_send, near_recv, local):
        self.n = count // 2
        self.x, self.out = x, out
        self.send, self.recv = send, recv
        self.near_send, self.near_recv, self.local = near_send, near_recv, local
        self.me, self.chip, self.core, self.partner = chip_place()
        self.there, self.source = chips(self.n)

    def relayed(self, k):
        return self.n == 4 and k == 3

    def far(self, k):
        src, slot = self.x, self.me
        if self.relayed(k):
            slot = self.source[1] * 2 + self.core
            src = self.out.at[slot]
        other = self.there[k] * 2 + self.core
        return remote(src, self.out.at[slot], self.send.at[k], self.recv.at[k], seq=other)

    def near(self, k):
        slot = self.source[k] * 2 + self.core
        src = self.x if k == 0 else self.out.at[slot]
        return remote(
            src, self.out.at[slot], self.near_send.at[k], self.near_recv.at[k], seq=self.partner
        )

    def start(self):
        for k in range(1, self.n):
            if not self.relayed(k):
                self.far(k).start()
        self.near(0).start()
        self.own = pltpu.make_async_copy(self.x, self.out.at[self.me], self.local)
        self.own.start()

    def arrive(self, k):
        self.far(k).wait_recv()
        if k == 1 and self.n == 4:
            self.far(3).start()
        self.near(k).start()

    def finish_far(self):
        for k in range(1, self.n):
            self.far(k).wait_send()
        for k in range(self.n):
            self.near(k).wait_send()

    def finish(self):
        self.own.wait()
        self.finish_far()
        for k in range(self.n):
            self.near(k).wait_recv()


class Scatter:
    def __init__(self, count, x, out, got, staged, arrived, send, recv, near_send, near_recv):
        self.n = count // 2
        self.x, self.out, self.got, self.staged, self.arrived = x, out, got, staged, arrived
        self.send, self.recv, self.near_send, self.near_recv = send, recv, near_send, near_recv
        self.me, self.chip, self.core, self.partner = chip_place()
        self.there, self.source = chips(self.n)
        self.relay = self.n == 4
        self.dest = self.source if self.relay else self.there
        self.order = [3, 1, 2, 0] if self.relay else list(range(1, self.n)) + [0]

    def near_slot(self, k):
        return self.dest[mate(self.n, k)] * 2 + 1 - self.core

    def own_slot(self, k):
        return self.dest[k] * 2 + self.core

    def near(self, k):
        return remote(
            self.x.at[self.near_slot(k)],
            self.got.at[k],
            self.near_send.at[k],
            self.near_recv.at[k],
            seq=self.partner,
        )

    def far(self, k):
        chip = self.there[1] if self.relay and k == 3 else self.there[k]
        return remote(
            self.staged.at[k],
            self.arrived.at[k],
            self.send.at[k],
            self.recv.at[k],
            seq=chip * 2 + self.core,
        )

    def start(self):
        for k in self.order:
            self.near(k).start()

    def exchange(self, k):
        slot = self.own_slot(k)
        self.near(k).wait_recv()
        hop = self.relay and k == 2
        if hop:
            self.far(3).wait_recv()

        def body(i, carry):
            rows = pl.ds(pl.multiple_of(i * CHUNK, CHUNK), CHUNK)
            total = self.x[slot, rows, :].astype(jnp.float32) + self.got[k, rows, :].astype(
                jnp.float32
            )
            if hop:
                total = total + self.arrived[3, rows, :].astype(jnp.float32)
            self.staged[k, rows, :] = total.astype(jnp.bfloat16)
            return carry

        lax.fori_loop(0, self.x.shape[1] // CHUNK, body, 0)
        if k:
            self.far(k).start()

    def finish(self):
        last = [1, 2] if self.relay else list(range(1, self.n))
        for k in last:
            self.far(k).wait_recv()

        def body(i, carry):
            rows = pl.ds(pl.multiple_of(i * CHUNK, CHUNK), CHUNK)
            total = self.staged[0, rows, :].astype(jnp.float32)
            for k in last:
                total = total + self.arrived[k, rows, :].astype(jnp.float32)
            self.out[rows, :] = total.astype(jnp.bfloat16)
            return carry

        lax.fori_loop(0, self.x.shape[1] // CHUNK, body, 0)
        for k in range(1, self.n):
            self.far(k).wait_send()
        for k in range(self.n):
            self.near(k).wait_send()


def gather_sems(n):
    return [DMA((n,)), DMA((n,)), DMA((n,)), DMA((n,)), DMA]


def scatter_scratch(count, shape):
    n = count // 2
    buffers = [pltpu.VMEM((n,) + shape, jnp.bfloat16) for unused in range(3)]
    return buffers + [DMA((n,)), DMA((n,)), DMA((n,)), DMA((n,))]


def params(number, mib=48):
    return pltpu.CompilerParams(
        collective_id=number, has_side_effects=True, vmem_limit_bytes=mib * 2**20
    )


def first_kernel(count, fs, grad_ref, w_ref, k_ref, v_ref, grad_out, k_out, v_out, head_out, *scratch):
    n = count // 2
    grad = Gather(count, grad_ref, grad_out, *scratch[:5])
    works = [
        Gather(count, k_ref, k_out, *scratch[5:10]),
        Gather(count, v_ref, v_out, *scratch[10:15]),
    ]
    part, parts, summed, z_send, z_recv, s_send, s_recv, local = scratch[15:]
    me = lax.axis_index("seq")
    mine = lax.axis_index("fsdp")
    rows = w_ref.shape[0] // fs
    greet(True, count, fs)

    def z_copy(k, step):
        other = lax.rem(mine + k, fs)
        pair = pl.ds(grad.source[step] * 2, 2)
        at = k * n + step
        return remote(
            part.at[other, pair], parts.at[k, pair], z_send.at[at], z_recv.at[at], fsdp=other
        )

    def s_copy(k):
        other = lax.rem(me + k, count)
        return remote(summed.at[other], head_out.at[me], s_send.at[k], s_recv.at[k], seq=other)

    def multiply(step):
        for half in range(2):
            slot = grad.source[step] * 2 + half
            product = lax.dot_general(
                w_ref[...],
                grad_out[slot],
                (((1,), (1,)), ((), ())),
                preferred_element_type=jnp.float32,
            )
            for f in range(fs):
                part[f, slot] = product[f * rows : (f + 1) * rows].astype(jnp.bfloat16)
        for k in range(1, fs):
            z_copy(k, step).start()

    grad.start()
    grad.own.wait()
    grad.near(0).wait_recv()
    multiply(0)
    for k in range(1, n):
        grad.arrive(k)
        if k == n - 1:
            for work in works:
                work.start()
        if k > 1:
            grad.near(mate(n, k - 1)).wait_recv()
            multiply(k - 1)
    grad.near(n - 1).wait_recv()
    multiply(n - 1)
    for k in range(1, n - 1):
        for work in works:
            work.arrive(k)
    for k in range(1, fs):
        for step in range(n):
            z_copy(k, step).wait_recv()

    def body(j, carry):
        total = part[mine, j].astype(jnp.float32)
        for k in range(1, fs):
            total = total + parts[k, j].astype(jnp.float32)
        summed[j] = total.astype(jnp.bfloat16)
        return carry

    lax.fori_loop(0, count, body, 0)
    for k in range(1, count):
        s_copy(k).start()
    own = pltpu.make_async_copy(summed.at[me], head_out.at[me], local)
    own.start()
    grad.finish_far()
    for work in works:
        work.arrive(n - 1)
    for work in works:
        work.finish()
    own.wait()
    for k in range(1, fs):
        for step in range(n):
            z_copy(k, step).wait_send()
    for k in range(1, count):
        s_copy(k).wait()


def first(count, fs, out_grad, weight, key_rows, value_rows):
    n = count // 2
    low = jnp.bfloat16
    slots = (count, weight.shape[0] // fs, out_grad.shape[0])
    return pl.pallas_call(
        functools.partial(first_kernel, count, fs),
        out_shape=[
            jax.ShapeDtypeStruct((count,) + out_grad.shape, low),
            jax.ShapeDtypeStruct((count,) + key_rows.shape, low),
            jax.ShapeDtypeStruct((count,) + key_rows.shape, low),
            jax.ShapeDtypeStruct(slots, low),
        ],
        in_specs=[ANY, VMEM, ANY, ANY],
        out_specs=[VMEM, ANY, ANY, ANY],
        scratch_shapes=gather_sems(n)
        + gather_sems(n)
        + gather_sems(n)
        + [
            pltpu.VMEM((fs,) + slots, low),
            pltpu.VMEM((fs,) + slots, low),
            pltpu.VMEM(slots, low),
            DMA((fs * n,)),
            DMA((fs * n,)),
            DMA((count,)),
            DMA((count,)),
            DMA,
        ],
        compiler_params=params(1, 61),
        name="gather_inputs_sum_head_grad",
    )(out_grad, weight, key_rows, value_rows)


def attend_kernel(blocks, pat, q_ref, k_ref, v_ref, g_ref, att_ref, qg_ref, kg_ref, vg_ref, *scratch):
    k_set, v_set, k_acc, v_acc = scratch
    scale = 1.0 / math.sqrt(HD)
    f32, low = jnp.float32, jnp.bfloat16
    k_acc[...] = jnp.zeros_like(k_acc)
    v_acc[...] = jnp.zeros_like(v_acc)
    nt = (((1,), (1,)), ((), ()))
    nn = (((1,), (0,)), ((), ()))
    tn = (((0,), (0,)), ((), ()))

    def dot(a, b, dims):
        return lax.dot_general(a, b, dims, preferred_element_type=f32)

    held = []
    for j in range(blocks):
        here = slice(j * BLK, (j + 1) * BLK)
        for s in range(NSEL):
            at = pl.ds(pl.multiple_of(pat[j, s] * BLK, BLK), BLK)
            k_set[j, s * BLK : (s + 1) * BLK, :] = k_ref[at, :]
            v_set[j, s * BLK : (s + 1) * BLK, :] = v_ref[at, :]
        held.append((here, dot(k_set[j], q_ref[here, :], nt) * scale))
    for j, (here, scores) in enumerate(held):
        q = q_ref[here, :]
        g = g_ref[:, here]
        prob_grad = dot(v_set[j], g, nn)
        top = jnp.max(scores, axis=0, keepdims=True)
        exps = jnp.exp(scores - top)
        probs = exps * (1.0 / jnp.sum(exps, axis=0, keepdims=True))
        probs_low = probs.astype(low)
        att_ref[:, here] = dot(v_set[j], probs_low, tn).astype(low)
        center = jnp.sum(probs * prob_grad, axis=0, keepdims=True)
        score_grad = (probs * (prob_grad - center)).astype(low)
        qg_ref[here, :] = (dot(score_grad, k_set[j], tn) * scale).astype(low)
        k_term = (dot(score_grad, q, nn) * scale).astype(low)
        v_term = dot(probs_low, g, nt).astype(low)
        for s in range(NSEL):
            at = pl.ds(pl.multiple_of(pat[j, s] * BLK, BLK), BLK)
            k_acc[at, :] += k_term[s * BLK : (s + 1) * BLK, :].astype(f32)
            v_acc[at, :] += v_term[s * BLK : (s + 1) * BLK, :].astype(f32)
    kg_ref[...] = k_acc[...].astype(low)
    vg_ref[...] = v_acc[...].astype(low)


def attend(pattern, queries, keys, values, grad_t):
    rows, width = queries.shape
    tokens = keys.shape[0]
    low = jnp.bfloat16
    by_col = lambda n: pl.BlockSpec((n, HD), lambda h, pat: (0, h))
    by_row = pl.BlockSpec((HD, rows), lambda h, pat: (h, 0))
    return pl.pallas_call(
        functools.partial(attend_kernel, rows // BLK),
        grid_spec=pltpu.PrefetchScalarGridSpec(
            num_scalar_prefetch=1,
            grid=(width // HD,),
            in_specs=[by_col(rows), by_col(tokens), by_col(tokens), by_row],
            out_specs=[by_row, by_col(rows), by_col(tokens), by_col(tokens)],
            scratch_shapes=[
                pltpu.VMEM((rows // BLK, NSEL * BLK, HD), low),
                pltpu.VMEM((rows // BLK, NSEL * BLK, HD), low),
                pltpu.VMEM((tokens, HD), jnp.float32),
                pltpu.VMEM((tokens, HD), jnp.float32),
            ],
        ),
        out_shape=[
            jax.ShapeDtypeStruct((width, rows), low),
            jax.ShapeDtypeStruct((rows, width), low),
            jax.ShapeDtypeStruct((tokens, width), low),
            jax.ShapeDtypeStruct((tokens, width), low),
        ],
        compiler_params=pltpu.CompilerParams(vmem_limit_bytes=48 * 2**20),
        name="attend",
    )(pattern, queries, keys, values, grad_t)


class Line:
    def __init__(self, fs, out, up_send, up_recv, down_send, down_recv):
        self.fs, self.out = fs, out
        self.up_sems, self.down_sems = (up_send, up_recv), (down_send, down_recv)
        self.mine = lax.axis_index("fsdp")

    def copy(self, sems, shard, step, other):
        slot = self.out.at[shard]
        return remote(slot, slot, sems[0].at[step], sems[1].at[step], fsdp=other)

    def sends(self, step, act):
        mine, end = self.mine, self.fs - 1

        @pl.when((mine >= step) & (mine < end))
        def up():
            act(self.copy(self.up_sems, mine - step, step, mine + 1))

        @pl.when((mine + step <= end) & (mine > 0))
        def down():
            act(self.copy(self.down_sems, mine + step, step, mine - 1))

    def start(self, step):
        self.sends(step, lambda copy: copy.start())

    def arrive(self, step):
        mine, end = self.mine, self.fs - 1

        @pl.when(mine - 1 >= step)
        def below():
            self.copy(self.up_sems, mine - 1 - step, step, mine - 1).wait_recv()

        @pl.when(mine + 1 + step <= end)
        def above():
            self.copy(self.down_sems, mine + 1 + step, step, mine + 1).wait_recv()

    def finish(self):
        for step in range(self.fs - 1):
            self.sends(step, lambda copy: copy.wait_send())


def late_kernel(count, fs, kg_ref, vg_ref, att_ref, k_out, v_out, att_out, *scratch):
    s_send, s_recv, local = scratch[14:17]
    line = Line(fs, att_out, *scratch[17:])
    me = lax.axis_index("seq")
    mine = lax.axis_index("fsdp")
    greet(True, count, fs)

    def s_copy(k):
        other = lax.rem(me + k, count)
        return remote(
            att_ref.at[other], att_out.at[mine, me], s_send.at[k], s_recv.at[k], seq=other
        )

    for k in range(1, count):
        s_copy(k).start()
    own = pltpu.make_async_copy(att_ref.at[me], att_out.at[mine, me], local)
    own.start()
    works = [
        Scatter(count, kg_ref, k_out, *scratch[:7]),
        Scatter(count, vg_ref, v_out, *scratch[7:14]),
    ]
    for work in works:
        work.start()
    order = works[0].order
    for work in works:
        work.exchange(order[0])
    own.wait()
    for k in range(1, count):
        s_copy(k).wait_recv()
    line.start(0)
    for i in range(1, max(len(order), fs)):
        if i < len(order):
            for work in works:
                work.exchange(order[i])
        if i < fs:
            line.arrive(i - 1)
            if i < fs - 1:
                line.start(i)
    for work in works:
        work.finish()
    for k in range(1, count):
        s_copy(k).wait_send()
    line.finish()


def late(count, fs, key_sums, value_sums, att):
    shape = key_sums.shape[1:]
    return pl.pallas_call(
        functools.partial(late_kernel, count, fs),
        out_shape=[
            jax.ShapeDtypeStruct(shape, jnp.bfloat16),
            jax.ShapeDtypeStruct(shape, jnp.bfloat16),
            jax.ShapeDtypeStruct((fs,) + att.shape, jnp.bfloat16),
        ],
        in_specs=[VMEM, VMEM, ANY],
        out_specs=[VMEM, VMEM, ANY],
        scratch_shapes=scatter_scratch(count, shape)
        + scatter_scratch(count, shape)
        + [DMA((count,)), DMA((count,)), DMA]
        + [DMA((fs,)) for unused in range(4)],
        compiler_params=params(3, 56),
        name="sum_key_value_grads_gather_attended",
    )(key_sums, value_sums, att)


def last_kernel(count, fs, part_e, att_ref, w_ref, grad_ref, out, weight_out, partial, flat, *scratch):
    greet(False, count, 0)
    work = Scatter(count, partial, out, *scratch)
    rows = out.shape[0]
    packed = att_ref.shape[2] % 16 == 0

    def multiply(slot):
        total = None
        if packed:
            total = lax.dot_general(
                att_ref[:, slot].reshape(fs * att_ref.shape[2], rows),
                w_ref[...].reshape(fs * att_ref.shape[2], w_ref.shape[2]),
                (((0,), (0,)), ((), ())),
                preferred_element_type=jnp.float32,
            )
        for f in range(0 if packed else fs):
            term = lax.dot_general(
                att_ref[f, slot],
                w_ref[f],
                (((0,), (0,)), ((), ())),
                preferred_element_type=jnp.float32,
            )
            total = term if total is None else total + term
        partial[slot] = total.astype(jnp.bfloat16)

    for k in work.order:
        multiply(work.near_slot(k))
        work.near(k).start()
    for k in work.order:
        multiply(work.own_slot(k))
        if k:
            work.exchange(k)

    def flatten(j, carry):
        at = pl.ds(pl.multiple_of(j * rows, rows), rows)
        for f in range(fs):
            flat[f, :, at] = att_ref[f, j]
        return carry

    lax.fori_loop(0, count, flatten, 0)

    def columns(i, carry):
        cols = pl.ds(pl.multiple_of(i * 256, 256), 256)
        for f in range(fs):
            product = jnp.dot(flat[f], grad_ref[:, cols], preferred_element_type=jnp.float32)
            if part_e % 8:
                weight_out[f, :, cols] = product
                continue
            heads = product.shape[0] // part_e
            for h in range(heads):
                weight_out[:, f * heads + h, cols] = product[h * part_e : (h + 1) * part_e]
        return carry

    lax.fori_loop(0, w_ref.shape[2] // 256, columns, 0)
    work.exchange(0)
    work.finish()


def last(count, part_e, att_all, weight, grad_all):
    fs, rows_here, cols = weight.shape
    tokens = grad_all.shape[0]
    shape = (tokens // count, cols)
    heads_all = fs * rows_here // part_e
    by_position = part_e % 8 == 0
    grad_shape = (part_e, heads_all, cols) if by_position else weight.shape
    projected, weight_grad = pl.pallas_call(
        functools.partial(last_kernel, count, fs, part_e),
        out_shape=[
            jax.ShapeDtypeStruct(shape, jnp.bfloat16),
            jax.ShapeDtypeStruct(grad_shape, jnp.float32),
        ],
        in_specs=[VMEM, VMEM, VMEM],
        out_specs=[VMEM, VMEM],
        scratch_shapes=[
            pltpu.VMEM((count,) + shape, jnp.bfloat16),
            pltpu.VMEM((fs, rows_here, tokens), jnp.bfloat16),
        ]
        + scatter_scratch(count, shape),
        compiler_params=params(4, 56),
        name="project_sum_weight_grad",
    )(att_all, weight, grad_all)
    if not by_position:
        weight_grad = weight_grad.reshape(heads_all, part_e, cols).transpose(1, 0, 2)
    return projected, weight_grad


def shards(count, fs, queries, key_rows, value_rows, pattern, out_weight, out_grad):
    rows, width = queries.shape
    heads = width // HD
    part_e, heads_all, cols = out_weight.shape
    tokens = rows * count
    weight = out_weight.transpose(1, 0, 2).reshape(heads_all * part_e, cols)

    grad_all, keys, values, head_grad = first(count, fs, out_grad, weight, key_rows, value_rows)
    grad_t = head_grad.reshape(count, heads, part_e, rows).transpose(1, 0, 2, 3)
    att_t, query_grad, key_sums, value_sums = attend(
        pattern,
        queries,
        keys.reshape(tokens, width),
        values.reshape(tokens, width),
        grad_t.reshape(width, rows),
    )
    att = att_t.reshape(heads, count, part_e, rows).transpose(1, 0, 2, 3)
    key_grad, value_grad, att_all = late(
        count,
        fs,
        key_sums.reshape(count, rows, width),
        value_sums.reshape(count, rows, width),
        att.reshape(count, heads * part_e, rows),
    )
    projected, weight_grad = last(
        count,
        part_e,
        att_all,
        weight.reshape(fs, heads * part_e, cols),
        grad_all.reshape(tokens, cols),
    )
    return (projected, query_grad, key_grad, value_grad, weight_grad)


def solution(mesh):
    placed = (
        P("seq", "fsdp"),
        P("seq", "fsdp"),
        P("seq", "fsdp"),
        P("seq", None),
        P("seq", None, "fsdp"),
        P("seq", "fsdp"),
    )
    return jax.shard_map(
        functools.partial(shards, mesh.shape["seq"], mesh.shape["fsdp"]),
        mesh=mesh,
        in_specs=placed,
        out_specs=(
            P("seq", "fsdp"),
            P("seq", "fsdp"),
            P("seq", "fsdp"),
            P("seq", "fsdp"),
            P("seq", None, "fsdp"),
        ),
        check_vma=False,
    )
```
